256 devices in a mesh: depth: 256 (over y, x, z, core).
Axes of the slice: x: 4, y: 4, z: 8, core: 2. Of those that a mesh axis runs over, the one named last changes fastest.
Arguments:
- weights: bfloat16 [256, 1024, 1024], P('depth'), may hold values from -0.1875 to 0.1875
- gains: float32 [256, 1024], P('depth'), may hold values from 0.1 to 1.9
- states: float32 [256, 512, 1024], P('depth'), may hold values from -1200 to 1200
- adjoints: float32 [256, 512, 1024], P('depth'), may hold values from -0.26516503 to 0.26516503
Outputs:
- grad_weight: bfloat16 [256, 1024, 1024], P('depth')
- grad_gain: float32 [256, 1024], P('depth')
The draws below stay inside these ranges and needn't reach their ends.
All inputs are finite; a program needn't handle non-finite values.
Results may differ from the reference program's by a relative error of at most 0.006.
Values sent between devices are 32-bit elements; how exact they have to be, the bound alone decides.
A program may use at most 64 MiB of HBM per device.

```python
import math
import jax
import jax.numpy as jnp
from jax import lax

D = 1024
TOK = 512
SWEEPS = 4
LAYERS = 256


def draw_states(key, part):
    first_key, second_key, third_key = jax.random.split(jax.random.fold_in(key, 17), 3)
    noise_vals = jnp.clip(jax.random.normal(first_key, (LAYERS, TOK, D), jnp.float32), -6.0, 6.0)
    upper_scale = 10.0
    row_scale = jnp.exp(jax.random.uniform(second_key, (LAYERS, TOK, 1), jnp.float32, 0.0, math.log(upper_scale)))
    col_scale = jnp.exp(jax.random.uniform(third_key, (LAYERS, 1, D), jnp.float32, 0.0, math.log(upper_scale)))
    return jnp.clip(noise_vals * row_scale * col_scale, -1200.0, 1200.0)


def levels(key, extent, pieces, low, top_value):
    def one(dim, blocks):
        draws = jax.random.uniform(jax.random.fold_in(jax.random.fold_in(key, 6), dim), (blocks,), jnp.float32, low / len(pieces), top_value / len(pieces))
        return jnp.repeat(jnp.exp(draws), extent[dim] // blocks).reshape((-1,) + (1,) * (len(extent) - dim - 1))

    level = one(*pieces[0])
    for cut in pieces[1:]:
        level = level * one(*cut)
    return level


def normal_values(rng, extent, deviation, reach, cuts=(), held_as=jnp.bfloat16):
    values = deviation * jax.random.normal(rng, extent, jnp.float32)
    if cuts:
        values = values * levels(rng, extent, cuts, -0.22, 0.18)
    return jnp.clip(values, -reach, reach).astype(held_as)


def setup_inputs(seed: int = 0) -> dict:
    streams_of = jax.random.split(jax.random.key(seed), 5)
    weights = normal_values(streams_of[0], (LAYERS, D, D), D ** -0.5, 0.1875, ((0, 256),))
    gains = jnp.clip(1.0 + 0.18 * jax.random.normal(streams_of[1], (LAYERS, D), jnp.float32), 0.1, 1.9)
    states = draw_states(jax.random.fold_in(streams_of[4], 71), 0)
    adjoints = normal_values(streams_of[3], (LAYERS, TOK, D), (TOK ** -0.5), 0.26516503, ((0, 256),), jnp.float32)
    return {"weights": weights, "gains": gains, "states": states, "adjoints": adjoints}


eps = 1e-06

def layer_terms(state, adjoint, gains, weights):
    inverse = lax.rsqrt(lax.optimization_barrier(jnp.mean(state * state, axis=-1, keepdims=True)) + eps)
    normed = state * inverse
    scaled = (normed * gains[:, None, :]).astype(jnp.bfloat16)
    preact = jnp.einsum('ltd,lde->lte', scaled.astype(jnp.float32), weights.astype(jnp.float32))
    squash = jax.nn.sigmoid(preact)
    output = state + preact * squash
    pre_grad = (adjoint * squash * (1.0 + preact * (1.0 - squash))).astype(jnp.bfloat16)
    feat_grad = jnp.einsum('lte,lde->ltd', pre_grad.astype(jnp.float32), weights.astype(jnp.float32))
    gained = feat_grad * gains[:, None, :]
    carried = adjoint + inverse * (gained - normed * lax.optimization_barrier(jnp.mean(gained * normed, axis=-1, keepdims=True)))
    return (output, carried, scaled, pre_grad, normed, feat_grad)

def reference(weights, gains, states, adjoints):
    state, adjoint = (states, adjoints)
    for sweep_index in range(SWEEPS):
        output, carried, scaled, pre_grad, normed, feat_grad = layer_terms(state, adjoint, gains, weights)
        state = jnp.concatenate([state[:1], output[:-1]], axis=0)
        adjoint = jnp.concatenate([carried[1:], adjoint[-1:]], axis=0)
    output, carried, scaled, pre_grad, normed, feat_grad = layer_terms(state, adjoint, gains, weights)
    grad_weight = jnp.einsum('ltd,lte->lde', scaled.astype(jnp.float32), pre_grad.astype(jnp.float32)).astype(jnp.bfloat16)
    grad_gain = lax.optimization_barrier(jnp.sum(normed * feat_grad, axis=1))
    return (grad_weight, grad_gain)
```

```python
import functools

import jax
import jax.numpy as jnp
from jax import lax
from jax.experimental import pallas as pl
from jax.experimental.pallas import tpu as pltpu
from jax.sharding import PartitionSpec as P

SWEEPS = 4
EPS = 1e-06
MESH = pl.DeviceIdType.MESH
CHUNKS = (64, 64, 128, 128, 64, 64)
TILE = 256


def kernel(
    n,
    weights_ref,
    gains_ref,
    states_ref,
    adjoints_ref,
    grad_weight_ref,
    grad_gain_ref,
    weights,
    gains,
    state,
    adjoint,
    state_out,
    adjoint_out,
    normed,
    slope,
    product,
    scaled,
    pre_grad,
    total,
    gain_total,
    result,
    load_sem,
    state_sem,
    adjoint_sem,
    state_send_sem,
    adjoint_send_sem,
    result_sem,
):
    me = lax.axis_index("depth")
    right, left = lax.rem(me + 1, n), lax.rem(me + n - 1, n)
    width = weights.shape[0]
    tiles = width // TILE
    starts = [sum(CHUNKS[:c]) for c in range(len(CHUNKS))]
    chunks = list(enumerate(zip(starts, CHUNKS)))

    barrier = pltpu.get_barrier_semaphore()
    for neighbour in (left, right):
        pl.semaphore_signal(barrier, inc=1, device_id=(neighbour,), device_id_type=MESH)

    def load_state(sweep, c):
        rows = pl.ds(starts[c], CHUNKS[c])
        return pltpu.make_async_copy(
            states_ref.at[0, rows], state.at[sweep, rows], state_sem.at[sweep, c]
        )

    def load_adjoint(sweep, c):
        rows = pl.ds(starts[c], CHUNKS[c])
        return pltpu.make_async_copy(
            adjoints_ref.at[0, rows], adjoint.at[sweep, rows], adjoint_sem.at[sweep, c]
        )

    def send_state(sweep, c):
        rows = pl.ds(starts[c], CHUNKS[c])
        slot = lax.rem(sweep, 2)
        return pltpu.make_async_remote_copy(
            src_ref=state_out.at[slot, rows],
            dst_ref=state.at[sweep + 1, rows],
            send_sem=state_send_sem.at[slot, c],
            recv_sem=state_sem.at[sweep + 1, c],
            device_id=(right,),
            device_id_type=MESH,
        )

    def send_adjoint(sweep, c):
        rows = pl.ds(starts[c], CHUNKS[c])
        slot = lax.rem(sweep, 2)
        return pltpu.make_async_remote_copy(
            src_ref=adjoint_out.at[slot, rows],
            dst_ref=adjoint.at[sweep + 1, rows],
            send_sem=adjoint_send_sem.at[slot, c],
            recv_sem=adjoint_sem.at[sweep + 1, c],
            device_id=(left,),
            device_id_type=MESH,
        )

    load_gains = pltpu.make_async_copy(gains_ref, gains, load_sem.at[0])
    load_gains.start()
    load_state(0, 0).start()
    load_weights = pltpu.make_async_copy(weights_ref.at[0], weights, load_sem.at[1])
    load_weights.start()
    for c, _ in chunks:
        if c:
            load_state(0, c).start()
        load_adjoint(0, c).start()

    @pl.when(me == 0)
    def _():
        for sweep in range(1, SWEEPS + 1):
            for c, _ in chunks:
                load_state(sweep, c).start()

    @pl.when(me == n - 1)
    def _():
        for sweep in range(1, SWEEPS + 1):
            for c, _ in chunks:
                load_adjoint(sweep, c).start()

    def forward(sweep, c, first, last):
        start, count = starts[c], CHUNKS[c]
        rows = pl.ds(start, count)
        load_state(sweep, c).wait()
        if first and c == 0:
            load_gains.wait()
        block = state[sweep, rows, :]
        inverse = lax.rsqrt(jnp.mean(block * block, axis=-1, keepdims=True) + EPS)
        unit = block * inverse
        normed[pl.ds(0, count), :] = unit
        scaled[rows, :] = (unit * gains[...]).astype(jnp.bfloat16)
        if first and c == 0:
            load_weights.wait()
        slot = lax.rem(sweep, 2)
        for t in range(tiles):
            columns = pl.ds(t * TILE, TILE)
            preact = jnp.dot(
                scaled[rows, :], weights[:, columns], preferred_element_type=jnp.float32
            )
            squash = 0.5 * jnp.tanh(0.5 * preact) + 0.5
            slope[pl.ds(0, count), columns] = squash * (1.0 + preact * (1.0 - squash))
            if not last:
                state_out[slot, rows, columns] = state[sweep, rows, columns] + preact * squash
        return inverse

    def backward(sweep, c, inverse, last):
        start, count = starts[c], CHUNKS[c]
        rows = pl.ds(start, count)
        here = pl.ds(0, count)
        load_adjoint(sweep, c).wait()
        pre_grad[rows, :] = (adjoint[sweep, rows, :] * slope[here, :]).astype(jnp.bfloat16)
        slot = lax.rem(sweep, 2)
        projection = jnp.zeros((count, 1), jnp.float32)
        for t in range(tiles):
            columns = pl.ds(t * TILE, TILE)
            feat_grad = lax.dot_general(
                pre_grad[rows, :],
                weights[columns, :],
                (((1,), (1,)), ((), ())),
                preferred_element_type=jnp.float32,
            )
            if last:
                part = jnp.sum(normed[here, columns] * feat_grad, axis=0, keepdims=True)
                gain_total[:, columns] = part if c == 0 else gain_total[:, columns] + part
            else:
                gained = feat_grad * gains[:, columns]
                product[here, columns] = gained
                projection += jnp.sum(gained * normed[here, columns], axis=-1, keepdims=True)
        if not last:
            projection = projection / width
            adjoint_out[slot, rows, :] = adjoint[sweep, rows, :] + inverse * (
                product[here, :] - normed[here, :] * projection
            )

    def sweep_chunk(sweep, c, first):
        if not isinstance(sweep, int) or sweep >= 2:

            @pl.when(jnp.logical_and(sweep >= 2, me < n - 1))
            def _():
                send_state(sweep - 2, c).wait_send()

            @pl.when(jnp.logical_and(sweep >= 2, me > 0))
            def _():
                send_adjoint(sweep - 2, c).wait_send()

        inverse = forward(sweep, c, first, False)
        if first and c == 0:
            pl.semaphore_wait(barrier, 2)

        @pl.when(me < n - 1)
        def _():
            send_state(sweep, c).start()

        backward(sweep, c, inverse, False)

        @pl.when(me > 0)
        def _():
            send_adjoint(sweep, c).start()

    for c, _ in chunks:
        sweep_chunk(0, c, True)

    @pl.loop(1, SWEEPS)
    def _(sweep):
        for c, _ in chunks:
            sweep_chunk(sweep, c, False)

    def store_result(t):
        columns = pl.ds(t * TILE, TILE)
        return pltpu.make_async_copy(
            result.at[columns], grad_weight_ref.at[0, columns], result_sem.at[t]
        )

    for c, (start, count) in chunks:
        rows = pl.ds(start, count)
        inverse = forward(SWEEPS, c, False, True)
        backward(SWEEPS, c, inverse, True)
        for t in range(tiles):
            columns = pl.ds(t * TILE, TILE)
            part = lax.dot_general(
                scaled[rows, columns],
                pre_grad[rows, :],
                (((0,), (0,)), ((), ())),
                preferred_element_type=jnp.float32,
            )
            if c == 0:
                total[columns, :] = part
            elif c < len(CHUNKS) - 1:
                total[columns, :] += part
            else:
                result[columns, :] = (total[columns, :] + part).astype(jnp.bfloat16)
                store_result(t).start()
    grad_gain_ref[...] = gain_total[...]

    for sweep in range(SWEEPS - 2, SWEEPS):
        for c, _ in chunks:

            @pl.when(me < n - 1)
            def _():
                send_state(sweep, c).wait_send()

            @pl.when(me > 0)
            def _():
                send_adjoint(sweep, c).wait_send()

    for t in range(tiles):
        store_result(t).wait()


def solution(mesh):
    n = mesh.shape["depth"]

    def step(weights, gains, states, adjoints):
        _, tokens, width = states.shape
        assert sum(CHUNKS) == tokens
        largest = max(CHUNKS)
        slots = pltpu.VMEM((SWEEPS + 1, tokens, width), jnp.float32)
        sent = pltpu.VMEM((2, tokens, width), jnp.float32)
        piece = pltpu.VMEM((largest, width), jnp.float32)
        whole = pltpu.VMEM((tokens, width), jnp.bfloat16)
        any_space = pl.BlockSpec(memory_space=pl.ANY)
        return pl.pallas_call(
            functools.partial(kernel, n),
            out_shape=(
                jax.ShapeDtypeStruct((1, width, width), jnp.bfloat16),
                jax.ShapeDtypeStruct((1, width), jnp.float32),
            ),
            in_specs=[any_space] * 4,
            out_specs=(any_space, pl.BlockSpec(memory_space=pltpu.VMEM)),
            scratch_shapes=[
                pltpu.VMEM((width, width), jnp.bfloat16),
                pltpu.VMEM((1, width), jnp.float32),
                slots,
                slots,
                sent,
                sent,
                piece,
                piece,
                piece,
                whole,
                whole,
                pltpu.VMEM((width, width), jnp.float32),
                pltpu.VMEM((1, width), jnp.float32),
                pltpu.VMEM((width, width), jnp.bfloat16),
                pltpu.SemaphoreType.DMA((2,)),
                pltpu.SemaphoreType.DMA((SWEEPS + 1, len(CHUNKS))),
                pltpu.SemaphoreType.DMA((SWEEPS + 1, len(CHUNKS))),
                pltpu.SemaphoreType.DMA((2, len(CHUNKS))),
                pltpu.SemaphoreType.DMA((2, len(CHUNKS))),
                pltpu.SemaphoreType.DMA((width // TILE,)),
            ],
            compiler_params=pltpu.CompilerParams(
                collective_id=0, has_side_effects=True, vmem_limit_bytes=56 * 2**20
            ),
            cost_estimate=pl.CostEstimate(
                flops=2 * tokens * width * width * (2 * SWEEPS + 3),
                bytes_accessed=4 * width * width + 8 * tokens * width,
                transcendentals=tokens * width * (SWEEPS + 1),
            ),
        )(weights, gains, states, adjoints)

    spec = P("depth", None, None)
    return jax.shard_map(
        step,
        mesh=mesh,
        in_specs=(spec, P("depth", None), spec, spec),
        out_specs=(spec, P("depth", None)),
        check_vma=False,
    )
```

```python
import functools

import jax
import jax.numpy as jnp
from jax import lax
from jax.experimental import pallas as pl
from jax.experimental.pallas import tpu as pltpu
from jax.sharding import PartitionSpec as P

SWEEPS = 4
EPS = 1e-06
MESH = pl.DeviceIdType.MESH
CHUNKS = (64, 128, 128, 128, 64)
TAIL = 64
STORE = 128
TILE = 256


def kernel(
    n,
    weights_ref,
    gains_ref,
    states_ref,
    adjoints_ref,
    total,
    scaled_tail,
    pre_grad_tail,
    gain_total,
    weights,
    gains,
    state,
    adjoint,
    state_out,
    adjoint_out,
    normed,
    slope,
    product,
    scaled,
    pre_grad,
    load_sem,
    state_sem,
    adjoint_sem,
    state_send_sem,
    adjoint_send_sem,
):
    me = lax.axis_index("depth")
    right, left = lax.rem(me + 1, n), lax.rem(me + n - 1, n)
    width = weights.shape[0]
    tokens = state.shape[1]
    tiles = width // TILE
    starts = [sum(CHUNKS[:c]) for c in range(len(CHUNKS))]
    chunks = list(enumerate(zip(starts, CHUNKS)))

    barrier = pltpu.get_barrier_semaphore()
    for neighbour in (left, right):
        pl.semaphore_signal(barrier, inc=1, device_id=(neighbour,), device_id_type=MESH)

    def load_state(sweep, c):
        rows = pl.ds(starts[c], CHUNKS[c])
        return pltpu.make_async_copy(
            states_ref.at[0, rows], state.at[sweep, rows], state_sem.at[sweep, c]
        )

    def load_adjoint(sweep, c):
        rows = pl.ds(starts[c], CHUNKS[c])
        return pltpu.make_async_copy(
            adjoints_ref.at[0, rows], adjoint.at[sweep, rows], adjoint_sem.at[sweep, c]
        )

    def send_state(sweep, c):
        rows = pl.ds(starts[c], CHUNKS[c])
        slot = lax.rem(sweep, 2)
        return pltpu.make_async_remote_copy(
            src_ref=state_out.at[slot, rows],
            dst_ref=state.at[sweep + 1, rows],
            send_sem=state_send_sem.at[slot, c],
            recv_sem=state_sem.at[sweep + 1, c],
            device_id=(right,),
            device_id_type=MESH,
        )

    def send_adjoint(sweep, c):
        rows = pl.ds(starts[c], CHUNKS[c])
        slot = lax.rem(sweep, 2)
        return pltpu.make_async_remote_copy(
            src_ref=adjoint_out.at[slot, rows],
            dst_ref=adjoint.at[sweep + 1, rows],
            send_sem=adjoint_send_sem.at[slot, c],
            recv_sem=adjoint_sem.at[sweep + 1, c],
            device_id=(left,),
            device_id_type=MESH,
        )

    def load_weights(t):
        rows = pl.ds(t * TILE, TILE)
        return pltpu.make_async_copy(
            weights_ref.at[0, rows], weights.at[rows], load_sem.at[1 + t]
        )

    load_gains = pltpu.make_async_copy(gains_ref, gains, load_sem.at[0])
    load_gains.start()
    load_state(0, 0).start()
    for t in range(tiles):
        load_weights(t).start()
    load_adjoint(0, 0).start()

    def load_the_rest():
        for c, _ in chunks[1:]:
            load_state(0, c).start()
            load_adjoint(0, c).start()

        @pl.when(me == 0)
        def _():
            for sweep in range(1, SWEEPS + 1):
                for c, _ in chunks:
                    load_state(sweep, c).start()

        @pl.when(me == n - 1)
        def _():
            for sweep in range(1, SWEEPS + 1):
                for c, _ in chunks:
                    load_adjoint(sweep, c).start()

    def forward(sweep, c, first, last):
        start, count = starts[c], CHUNKS[c]
        rows = pl.ds(start, count)
        load_state(sweep, c).wait()
        if first and c == 0:
            load_gains.wait()
        block = state[sweep, rows, :]
        inverse = lax.rsqrt(jnp.mean(block * block, axis=-1, keepdims=True) + EPS)
        unit = block * inverse
        normed[pl.ds(0, count), :] = unit
        scaled[rows, :] = (unit * gains[...]).astype(jnp.bfloat16)
        if first and c == 0:
            for t in range(tiles):
                load_weights(t).wait()
            load_the_rest()
        slot = lax.rem(sweep, 2)
        for t in range(tiles):
            columns = pl.ds(t * TILE, TILE)
            preact = jnp.dot(
                scaled[rows, :], weights[:, columns], preferred_element_type=jnp.float32
            )
            squash = 0.5 * jnp.tanh(0.5 * preact) + 0.5
            slope[pl.ds(0, count), columns] = squash * (1.0 + preact * (1.0 - squash))
            if not last:
                state_out[slot, rows, columns] = state[sweep, rows, columns] + preact * squash
        return inverse

    def backward(sweep, c, inverse, last):
        start, count = starts[c], CHUNKS[c]
        rows = pl.ds(start, count)
        here = pl.ds(0, count)
        load_adjoint(sweep, c).wait()
        pre_grad[rows, :] = (adjoint[sweep, rows, :] * slope[here, :]).astype(jnp.bfloat16)
        slot = lax.rem(sweep, 2)
        projection = jnp.zeros((count, 1), jnp.float32)
        for t in range(tiles):
            columns = pl.ds(t * TILE, TILE)
            feat_grad = lax.dot_general(
                pre_grad[rows, :],
                weights[columns, :],
                (((1,), (1,)), ((), ())),
                preferred_element_type=jnp.float32,
            )
            if last:
                part = jnp.sum(normed[here, columns] * feat_grad, axis=0, keepdims=True)
                gain_total[:, columns] = part if c == 0 else gain_total[:, columns] + part
            else:
                gained = feat_grad * gains[:, columns]
                product[here, columns] = gained
                projection += jnp.sum(gained * normed[here, columns], axis=-1, keepdims=True)
        if not last:
            projection = projection / width
            adjoint_out[slot, rows, :] = adjoint[sweep, rows, :] + inverse * (
                product[here, :] - normed[here, :] * projection
            )

    def sweep_chunk(sweep, c, first):
        if not isinstance(sweep, int) or sweep >= 2:

            @pl.when(jnp.logical_and(sweep >= 2, me < n - 1))
            def _():
                send_state(sweep - 2, c).wait_send()

            @pl.when(jnp.logical_and(sweep >= 2, me > 0))
            def _():
                send_adjoint(sweep - 2, c).wait_send()

        inverse = forward(sweep, c, first, False)
        if first and c == 0:
            pl.semaphore_wait(barrier, 2)

        @pl.when(me < n - 1)
        def _():
            send_state(sweep, c).start()

        backward(sweep, c, inverse, False)

        @pl.when(me > 0)
        def _():
            send_adjoint(sweep, c).start()

    for c, _ in chunks:
        sweep_chunk(0, c, True)

    @pl.loop(1, SWEEPS)
    def _(sweep):
        for c, _ in chunks:
            sweep_chunk(sweep, c, False)

    for c, (start, count) in chunks:
        rows = pl.ds(start, count)
        inverse = forward(SWEEPS, c, False, True)
        backward(SWEEPS, c, inverse, True)
        if start >= tokens - TAIL:
            here = pl.ds(start - (tokens - TAIL), count)
            scaled_tail[here, :] = scaled[rows, :]
            pre_grad_tail[here, :] = pre_grad[rows, :]
        else:
            for t in range(tiles):
                columns = pl.ds(t * TILE, TILE)
                part = lax.dot_general(
                    scaled[rows, columns],
                    pre_grad[rows, :],
                    (((0,), (0,)), ((), ())),
                    preferred_element_type=jnp.float32,
                )
                total[columns, :] = part if c == 0 else total[columns, :] + part

    for sweep in range(SWEEPS - 2, SWEEPS):
        for c, _ in chunks:

            @pl.when(me < n - 1)
            def _():
                send_state(sweep, c).wait_send()

            @pl.when(me > 0)
            def _():
                send_adjoint(sweep, c).wait_send()


def finish(
    total,
    scaled_tail,
    pre_grad_tail,
    gain_total,
    grad_weight_ref,
    grad_gain_ref,
    result,
    result_sem,
    gain_sem,
):
    store_gain = pltpu.make_async_copy(gain_total, grad_gain_ref, gain_sem)
    store_gain.start()
    stores = []
    for t in range(total.shape[0] // STORE):
        columns = pl.ds(t * STORE, STORE)
        part = lax.dot_general(
            scaled_tail[:, columns],
            pre_grad_tail[...],
            (((0,), (0,)), ((), ())),
            preferred_element_type=jnp.float32,
        )
        result[columns, :] = (total[columns, :] + part).astype(jnp.bfloat16)
        store = pltpu.make_async_copy(
            result.at[columns], grad_weight_ref.at[0, columns], result_sem.at[t]
        )
        store.start()
        stores.append(store)
    for store in stores:
        store.wait()
    store_gain.wait()


def solution(mesh):
    n = mesh.shape["depth"]

    def step(weights, gains, states, adjoints):
        _, tokens, width = states.shape
        assert sum(CHUNKS) == tokens
        largest = max(CHUNKS)
        slots = pltpu.VMEM((SWEEPS + 1, tokens, width), jnp.float32)
        sent = pltpu.VMEM((2, tokens, width), jnp.float32)
        piece = pltpu.VMEM((largest, width), jnp.float32)
        whole = pltpu.VMEM((tokens, width), jnp.bfloat16)
        any_space = pl.BlockSpec(memory_space=pl.ANY)
        vmem = pl.BlockSpec(memory_space=pltpu.VMEM)
        parts = pl.pallas_call(
            functools.partial(kernel, n),
            out_shape=(
                pltpu.VMEM((width, width), jnp.float32),
                pltpu.VMEM((TAIL, width), jnp.bfloat16),
                pltpu.VMEM((TAIL, width), jnp.bfloat16),
                pltpu.VMEM((1, width), jnp.float32),
            ),
            in_specs=[pl.BlockSpec(memory_space=pltpu.HBM)] * 4,
            out_specs=(vmem,) * 4,
            scratch_shapes=[
                pltpu.VMEM((width, width), jnp.bfloat16),
                pltpu.VMEM((1, width), jnp.float32),
                slots,
                slots,
                sent,
                sent,
                piece,
                piece,
                piece,
                whole,
                whole,
                pltpu.SemaphoreType.DMA((1 + width // TILE,)),
                pltpu.SemaphoreType.DMA((SWEEPS + 1, len(CHUNKS))),
                pltpu.SemaphoreType.DMA((SWEEPS + 1, len(CHUNKS))),
                pltpu.SemaphoreType.DMA((2, len(CHUNKS))),
                pltpu.SemaphoreType.DMA((2, len(CHUNKS))),
            ],
            compiler_params=pltpu.CompilerParams(
                collective_id=0, has_side_effects=True, vmem_limit_bytes=48 * 2**20
            ),
            cost_estimate=pl.CostEstimate(
                flops=2 * tokens * width * width * (2 * SWEEPS + 3),
                bytes_accessed=4 * width * width + 8 * tokens * width,
                transcendentals=tokens * width * (SWEEPS + 1),
            ),
        )(*(pltpu.with_memory_space_constraint(x, pltpu.HBM) for x in (weights, gains, states, adjoints)))
        return pl.pallas_call(
            finish,
            out_shape=(
                jax.ShapeDtypeStruct((1, width, width), jnp.bfloat16),
                jax.ShapeDtypeStruct((1, width), jnp.float32),
            ),
            in_specs=[vmem] * 4,
            out_specs=(any_space, any_space),
            scratch_shapes=[
                pltpu.VMEM((width, width), jnp.bfloat16),
                pltpu.SemaphoreType.DMA((width // STORE,)),
                pltpu.SemaphoreType.DMA,
            ],
            compiler_params=pltpu.CompilerParams(vmem_limit_bytes=24 * 2**20),
            cost_estimate=pl.CostEstimate(
                flops=2 * TAIL * width * width,
                bytes_accessed=6 * width * width,
                transcendentals=0,
            ),
        )(*parts)

    spec = P("depth", None, None)
    return jax.shard_map(
        step,
        mesh=mesh,
        in_specs=(spec, P("depth", None), spec, spec),
        out_specs=(spec, P("depth", None)),
        check_vma=False,
    )
```

```python
import functools

import jax
import jax.numpy as jnp
from jax import lax
from jax.experimental import pallas as pl
from jax.experimental.pallas import tpu as pltpu
from jax.sharding import PartitionSpec as P

SWEEPS = 4
EPS = 1e-06
MESH = pl.DeviceIdType.MESH
CHUNKS = (64, 128, 128, 128, 64)
TAIL = 64
COLUMN = 16
ROW = 4
FIRST_RELAY = 9
SECOND_RELAY = 3
FIRST_AFTER = 1
SECOND_AFTER = 2
DETOUR = 32
DETOUR_CHUNK = 3
STORE = 128
TILE = 256


def kernel(
    n,
    weights_ref,
    gains_ref,
    states_ref,
    adjoints_ref,
    total,
    scaled_tail,
    pre_grad_tail,
    gain_total,
    weights,
    gains,
    state,
    adjoint,
    state_out,
    adjoint_out,
    normed,
    slope,
    product,
    scaled,
    pre_grad,
    load_sem,
    state_sem,
    adjoint_sem,
    state_send_sem,
    adjoint_send_sem,
    relay,
    relay_sem,
    relay_send_sem,
):
    me = lax.axis_index("depth")
    right, left = lax.rem(me + 1, n), lax.rem(me + n - 1, n)
    width = weights.shape[0]
    tokens = state.shape[1]
    tiles = width // TILE
    starts = [sum(CHUNKS[:c]) for c in range(len(CHUNKS))]
    chunks = list(enumerate(zip(starts, CHUNKS)))

    column, place = me // COLUMN, lax.rem(me, COLUMN)
    crosses = jnp.logical_and(lax.rem(column, ROW) == ROW - 1, column < n // COLUMN - 1)
    crossed = jnp.logical_and(lax.rem(column, ROW) == 0, column > 0)
    diverts = jnp.logical_and(crosses, place == COLUMN - 1)
    relays_first = jnp.logical_and(crosses, place == FIRST_RELAY)
    relays_second = jnp.logical_and(crossed, place == SECOND_RELAY)
    ends = jnp.logical_and(crossed, place == 0)
    first_relay = lax.rem(me + n - (COLUMN - 1 - FIRST_RELAY), n)
    second_relay = lax.rem(me + COLUMN - (FIRST_RELAY - SECOND_RELAY), n)
    end = lax.rem(me + n - SECOND_RELAY, n)

    barrier = pltpu.get_barrier_semaphore()
    for neighbour in (left, right):
        pl.semaphore_signal(barrier, inc=1, device_id=(neighbour,), device_id_type=MESH)
    for receives, sender in (
        (relays_first, lax.rem(me + COLUMN - 1 - FIRST_RELAY, n)),
        (relays_second, lax.rem(me + n - COLUMN + FIRST_RELAY - SECOND_RELAY, n)),
        (ends, lax.rem(me + SECOND_RELAY, n)),
    ):

        @pl.when(receives)
        def _():
            pl.semaphore_signal(barrier, inc=1, device_id=(sender,), device_id_type=MESH)

    def load_state(sweep, c):
        rows = pl.ds(starts[c], CHUNKS[c])
        return pltpu.make_async_copy(
            states_ref.at[0, rows], state.at[sweep, rows], state_sem.at[sweep, c]
        )

    def load_adjoint(sweep, c):
        rows = pl.ds(starts[c], CHUNKS[c])
        return pltpu.make_async_copy(
            adjoints_ref.at[0, rows], adjoint.at[sweep, rows], adjoint_sem.at[sweep, c]
        )

    def send_state(sweep, c):
        rows = pl.ds(starts[c], CHUNKS[c])
        slot = lax.rem(sweep, 2)
        return pltpu.make_async_remote_copy(
            src_ref=state_out.at[slot, rows],
            dst_ref=state.at[sweep + 1, rows],
            send_sem=state_send_sem.at[slot, c],
            recv_sem=state_sem.at[sweep + 1, c],
            device_id=(right,),
            device_id_type=MESH,
        )

    def send_state_tile(c, t):
        rows = pl.ds(starts[c], CHUNKS[c])
        columns = pl.ds(t * TILE, TILE)
        return pltpu.make_async_remote_copy(
            src_ref=state_out.at[0, rows, columns],
            dst_ref=state.at[1, rows, columns],
            send_sem=state_send_sem.at[0, c],
            recv_sem=state_sem.at[1, c],
            device_id=(right,),
            device_id_type=MESH,
        )

    detour_start = starts[DETOUR_CHUNK] + CHUNKS[DETOUR_CHUNK] - DETOUR
    detour = pl.ds(detour_start, DETOUR)

    def send_direct():
        rows = pl.ds(starts[DETOUR_CHUNK], CHUNKS[DETOUR_CHUNK] - DETOUR)
        return pltpu.make_async_remote_copy(
            src_ref=state_out.at[0, rows],
            dst_ref=state.at[1, rows],
            send_sem=state_send_sem.at[0, DETOUR_CHUNK],
            recv_sem=state_sem.at[1, DETOUR_CHUNK],
            device_id=(right,),
            device_id_type=MESH,
        )

    def send_detour():
        return pltpu.make_async_remote_copy(
            src_ref=state_out.at[0, detour],
            dst_ref=relay,
            send_sem=state_send_sem.at[0, DETOUR_CHUNK],
            recv_sem=relay_sem,
            device_id=(first_relay,),
            device_id_type=MESH,
        )

    def pass_on():
        return pltpu.make_async_remote_copy(
            src_ref=relay,
            dst_ref=relay,
            send_sem=relay_send_sem,
            recv_sem=relay_sem,
            device_id=(second_relay,),
            device_id_type=MESH,
        )

    def deliver():
        return pltpu.make_async_remote_copy(
            src_ref=relay,
            dst_ref=state.at[1, detour],
            send_sem=relay_send_sem,
            recv_sem=state_sem.at[1, DETOUR_CHUNK],
            device_id=(end,),
            device_id_type=MESH,
        )

    def send_adjoint(sweep, c):
        rows = pl.ds(starts[c], CHUNKS[c])
        slot = lax.rem(sweep, 2)
        return pltpu.make_async_remote_copy(
            src_ref=adjoint_out.at[slot, rows],
            dst_ref=adjoint.at[sweep + 1, rows],
            send_sem=adjoint_send_sem.at[slot, c],
            recv_sem=adjoint_sem.at[sweep + 1, c],
            device_id=(left,),
            device_id_type=MESH,
        )

    def load_weights(t):
        rows = pl.ds(t * TILE, TILE)
        return pltpu.make_async_copy(
            weights_ref.at[0, rows], weights.at[rows], load_sem.at[1 + t]
        )

    load_gains = pltpu.make_async_copy(gains_ref, gains, load_sem.at[0])
    load_gains.start()
    load_state(0, 0).start()
    for t in range(tiles):
        load_weights(t).start()
    load_adjoint(0, 0).start()

    def load_the_rest():
        for c, _ in chunks[1:]:
            load_state(0, c).start()
            load_adjoint(0, c).start()

        @pl.when(me == 0)
        def _():
            for sweep in range(1, SWEEPS + 1):
                for c, _ in chunks:
                    load_state(sweep, c).start()

        @pl.when(me == n - 1)
        def _():
            for sweep in range(1, SWEEPS + 1):
                for c, _ in chunks:
                    load_adjoint(sweep, c).start()

    def forward(sweep, c, first, last):
        start, count = starts[c], CHUNKS[c]
        rows = pl.ds(start, count)
        load_state(sweep, c).wait()
        if first and c == 0:
            load_gains.wait()
        block = state[sweep, rows, :]
        inverse = lax.rsqrt(jnp.mean(block * block, axis=-1, keepdims=True) + EPS)
        unit = block * inverse
        normed[pl.ds(0, count), :] = unit
        scaled[rows, :] = (unit * gains[...]).astype(jnp.bfloat16)
        if first and c == 0:
            for t in range(tiles):
                load_weights(t).wait()
            load_the_rest()
        slot = lax.rem(sweep, 2)
        for t in range(tiles):
            columns = pl.ds(t * TILE, TILE)
            preact = jnp.dot(
                scaled[rows, :], weights[:, columns], preferred_element_type=jnp.float32
            )
            squash = 0.5 * jnp.tanh(0.5 * preact) + 0.5
            slope[pl.ds(0, count), columns] = squash * (1.0 + preact * (1.0 - squash))
            if not last:
                state_out[slot, rows, columns] = state[sweep, rows, columns] + preact * squash
            if first and c == 0:
                if t == 0:
                    more = jnp.logical_or(diverts, jnp.logical_or(relays_first, relays_second))
                    pl.semaphore_wait(barrier, jnp.where(more, 3, 2))

                @pl.when(me < n - 1)
                def _():
                    send_state_tile(c, t).start()
        return inverse

    def backward(sweep, c, inverse, last):
        start, count = starts[c], CHUNKS[c]
        rows = pl.ds(start, count)
        here = pl.ds(0, count)
        load_adjoint(sweep, c).wait()
        pre_grad[rows, :] = (adjoint[sweep, rows, :] * slope[here, :]).astype(jnp.bfloat16)
        slot = lax.rem(sweep, 2)
        projection = jnp.zeros((count, 1), jnp.float32)
        for t in range(tiles):
            columns = pl.ds(t * TILE, TILE)
            feat_grad = lax.dot_general(
                pre_grad[rows, :],
                weights[columns, :],
                (((1,), (1,)), ((), ())),
                preferred_element_type=jnp.float32,
            )
            if last:
                part = jnp.sum(normed[here, columns] * feat_grad, axis=0, keepdims=True)
                gain_total[:, columns] = part if c == 0 else gain_total[:, columns] + part
            else:
                gained = feat_grad * gains[:, columns]
                product[here, columns] = gained
                projection += jnp.sum(gained * normed[here, columns], axis=-1, keepdims=True)
        if not last:
            projection = projection / width
            adjoint_out[slot, rows, :] = adjoint[sweep, rows, :] + inverse * (
                product[here, :] - normed[here, :] * projection
            )

    def sweep_chunk(sweep, c, first):
        if not isinstance(sweep, int) or sweep >= 2:

            @pl.when(jnp.logical_and(sweep >= 2, me < n - 1))
            def _():
                send_state(sweep - 2, c).wait_send()

            @pl.when(jnp.logical_and(sweep >= 2, me > 0))
            def _():
                send_adjoint(sweep - 2, c).wait_send()

        inverse = forward(sweep, c, first, False)
        if first and c == DETOUR_CHUNK:

            @pl.when(diverts)
            def _():
                send_direct().start()
                send_detour().start()

            @pl.when(jnp.logical_and(me < n - 1, jnp.logical_not(diverts)))
            def _():
                send_state(sweep, c).start()

        elif not (first and c == 0):

            @pl.when(me < n - 1)
            def _():
                send_state(sweep, c).start()

        backward(sweep, c, inverse, False)

        @pl.when(me > 0)
        def _():
            send_adjoint(sweep, c).start()

    for c, _ in chunks:
        sweep_chunk(0, c, True)

    @pl.loop(1, SWEEPS)
    def _(sweep):
        for c, _ in chunks:
            sweep_chunk(sweep, c, False)
            if c == FIRST_AFTER:

                @pl.when(jnp.logical_and(sweep == 1, relays_first))
                def _():
                    pass_on().wait_recv()
                    pass_on().start()

            if c == SECOND_AFTER:

                @pl.when(jnp.logical_and(sweep == 1, relays_second))
                def _():
                    pass_on().wait_recv()
                    deliver().start()


    for c, (start, count) in chunks:
        rows = pl.ds(start, count)
        inverse = forward(SWEEPS, c, False, True)
        backward(SWEEPS, c, inverse, True)
        if start >= tokens - TAIL:
            here = pl.ds(start - (tokens - TAIL), count)
            scaled_tail[here, :] = scaled[rows, :]
            pre_grad_tail[here, :] = pre_grad[rows, :]
        else:
            for t in range(tiles):
                columns = pl.ds(t * TILE, TILE)
                part = lax.dot_general(
                    scaled[rows, columns],
                    pre_grad[rows, :],
                    (((0,), (0,)), ((), ())),
                    preferred_element_type=jnp.float32,
                )
                total[columns, :] = part if c == 0 else total[columns, :] + part

    @pl.when(relays_first)
    def _():
        pass_on().wait_send()

    @pl.when(relays_second)
    def _():
        deliver().wait_send()

    for sweep in range(SWEEPS - 2, SWEEPS):
        for c, _ in chunks:

            @pl.when(me < n - 1)
            def _():
                send_state(sweep, c).wait_send()

            @pl.when(me > 0)
            def _():
                send_adjoint(sweep, c).wait_send()


def finish(
    total,
    scaled_tail,
    pre_grad_tail,
    gain_total,
    grad_weight_ref,
    grad_gain_ref,
    result,
    result_sem,
    gain_sem,
):
    store_gain = pltpu.make_async_copy(gain_total, grad_gain_ref, gain_sem)
    store_gain.start()
    stores = []
    for t in range(total.shape[0] // STORE):
        columns = pl.ds(t * STORE, STORE)
        part = lax.dot_general(
            scaled_tail[:, columns],
            pre_grad_tail[...],
            (((0,), (0,)), ((), ())),
            preferred_element_type=jnp.float32,
        )
        result[columns, :] = (total[columns, :] + part).astype(jnp.bfloat16)
        store = pltpu.make_async_copy(
            result.at[columns], grad_weight_ref.at[0, columns], result_sem.at[t]
        )
        store.start()
        stores.append(store)
    for store in stores:
        store.wait()
    store_gain.wait()


def solution(mesh):
    n = mesh.shape["depth"]

    def step(weights, gains, states, adjoints):
        _, tokens, width = states.shape
        assert sum(CHUNKS) == tokens
        largest = max(CHUNKS)
        slots = pltpu.VMEM((SWEEPS + 1, tokens, width), jnp.float32)
        sent = pltpu.VMEM((2, tokens, width), jnp.float32)
        piece = pltpu.VMEM((largest, width), jnp.float32)
        whole = pltpu.VMEM((tokens, width), jnp.bfloat16)
        any_space = pl.BlockSpec(memory_space=pl.ANY)
        vmem = pl.BlockSpec(memory_space=pltpu.VMEM)
        parts = pl.pallas_call(
            functools.partial(kernel, n),
            out_shape=(
                pltpu.VMEM((width, width), jnp.float32),
                pltpu.VMEM((TAIL, width), jnp.bfloat16),
                pltpu.VMEM((TAIL, width), jnp.bfloat16),
                pltpu.VMEM((1, width), jnp.float32),
            ),
            in_specs=[pl.BlockSpec(memory_space=pltpu.HBM)] * 4,
            out_specs=(vmem,) * 4,
            scratch_shapes=[
                pltpu.VMEM((width, width), jnp.bfloat16),
                pltpu.VMEM((1, width), jnp.float32),
                slots,
                slots,
                sent,
                sent,
                piece,
                piece,
                piece,
                whole,
                whole,
                pltpu.SemaphoreType.DMA((1 + width // TILE,)),
                pltpu.SemaphoreType.DMA((SWEEPS + 1, len(CHUNKS))),
                pltpu.SemaphoreType.DMA((SWEEPS + 1, len(CHUNKS))),
                pltpu.SemaphoreType.DMA((2, len(CHUNKS))),
                pltpu.SemaphoreType.DMA((2, len(CHUNKS))),
                pltpu.VMEM((DETOUR, width), jnp.float32),
                pltpu.SemaphoreType.DMA,
                pltpu.SemaphoreType.DMA,
            ],
            compiler_params=pltpu.CompilerParams(
                collective_id=0, has_side_effects=True, vmem_limit_bytes=48 * 2**20
            ),
            cost_estimate=pl.CostEstimate(
                flops=2 * tokens * width * width * (2 * SWEEPS + 3),
                bytes_accessed=4 * width * width + 8 * tokens * width,
                transcendentals=tokens * width * (SWEEPS + 1),
            ),
        )(*(pltpu.with_memory_space_constraint(x, pltpu.HBM) for x in (weights, gains, states, adjoints)))
        return pl.pallas_call(
            finish,
            out_shape=(
                jax.ShapeDtypeStruct((1, width, width), jnp.bfloat16),
                jax.ShapeDtypeStruct((1, width), jnp.float32),
            ),
            in_specs=[vmem] * 4,
            out_specs=(any_space, any_space),
            scratch_shapes=[
                pltpu.VMEM((width, width), jnp.bfloat16),
                pltpu.SemaphoreType.DMA((width // STORE,)),
                pltpu.SemaphoreType.DMA,
            ],
            compiler_params=pltpu.CompilerParams(vmem_limit_bytes=24 * 2**20),
            cost_estimate=pl.CostEstimate(
                flops=2 * TAIL * width * width,
                bytes_accessed=6 * width * width,
                transcendentals=0,
            ),
        )(*parts)

    spec = P("depth", None, None)
    return jax.shard_map(
        step,
        mesh=mesh,
        in_specs=(spec, P("depth", None), spec, spec),
        out_specs=(spec, P("depth", None)),
        check_vma=False,
    )
```

```python
import functools

import jax
import jax.numpy as jnp
from jax import lax
from jax.experimental import pallas as pl
from jax.experimental.pallas import tpu as pltpu
from jax.sharding import PartitionSpec as P

SWEEPS = 4
EPS = 1e-06
MESH = pl.DeviceIdType.MESH
CHUNKS = (64, 192, 192, 64)
TAIL = 64
COLUMN = 16
ROW = 4
FIRST_RELAY = 9
SECOND_RELAY = 3
FIRST_AFTER = 1
SECOND_AFTER = 1
DETOUR = 32
DETOUR_CHUNK = 2
STORE = 128
TILE = 256


def kernel(
    n,
    weights_ref,
    gains_ref,
    states_ref,
    adjoints_ref,
    total,
    scaled_tail,
    pre_grad_tail,
    gain_total,
    weights,
    gains,
    state,
    adjoint,
    state_out,
    adjoint_out,
    normed,
    slope,
    product,
    scaled,
    pre_grad,
    load_sem,
    state_sem,
    adjoint_sem,
    state_send_sem,
    adjoint_send_sem,
    relay,
    relay_sem,
    relay_send_sem,
):
    me = lax.axis_index("depth")
    right, left = lax.rem(me + 1, n), lax.rem(me + n - 1, n)
    width = weights.shape[0]
    tokens = state.shape[1]
    tiles = width // TILE
    starts = [sum(CHUNKS[:c]) for c in range(len(CHUNKS))]
    chunks = list(enumerate(zip(starts, CHUNKS)))

    column, place = me // COLUMN, lax.rem(me, COLUMN)
    crosses = jnp.logical_and(lax.rem(column, ROW) == ROW - 1, column < n // COLUMN - 1)
    crossed = jnp.logical_and(lax.rem(column, ROW) == 0, column > 0)
    diverts = jnp.logical_and(crosses, place == COLUMN - 1)
    relays_first = jnp.logical_and(crosses, place == FIRST_RELAY)
    relays_second = jnp.logical_and(crossed, place == SECOND_RELAY)
    ends = jnp.logical_and(crossed, place == 0)
    first_relay = lax.rem(me + n - (COLUMN - 1 - FIRST_RELAY), n)
    second_relay = lax.rem(me + COLUMN - (FIRST_RELAY - SECOND_RELAY), n)
    end = lax.rem(me + n - SECOND_RELAY, n)

    barrier = pltpu.get_barrier_semaphore()
    for neighbour in (left, right):
        pl.semaphore_signal(barrier, inc=1, device_id=(neighbour,), device_id_type=MESH)
    for receives, sender in (
        (relays_first, lax.rem(me + COLUMN - 1 - FIRST_RELAY, n)),
        (relays_second, lax.rem(me + n - COLUMN + FIRST_RELAY - SECOND_RELAY, n)),
        (ends, lax.rem(me + SECOND_RELAY, n)),
    ):

        @pl.when(receives)
        def _():
            pl.semaphore_signal(barrier, inc=1, device_id=(sender,), device_id_type=MESH)

    def load_state(sweep, c):
        rows = pl.ds(starts[c], CHUNKS[c])
        return pltpu.make_async_copy(
            states_ref.at[0, rows], state.at[sweep, rows], state_sem.at[sweep, c]
        )

    def load_adjoint(sweep, c):
        rows = pl.ds(starts[c], CHUNKS[c])
        return pltpu.make_async_copy(
            adjoints_ref.at[0, rows], adjoint.at[sweep, rows], adjoint_sem.at[sweep, c]
        )

    def send_state(sweep, c):
        rows = pl.ds(starts[c], CHUNKS[c])
        slot = lax.rem(sweep, 2)
        return pltpu.make_async_remote_copy(
            src_ref=state_out.at[slot, rows],
            dst_ref=state.at[sweep + 1, rows],
            send_sem=state_send_sem.at[slot, c],
            recv_sem=state_sem.at[sweep + 1, c],
            device_id=(right,),
            device_id_type=MESH,
        )

    def send_state_tile(c, t):
        rows = pl.ds(starts[c], CHUNKS[c])
        columns = pl.ds(t * TILE, TILE)
        return pltpu.make_async_remote_copy(
            src_ref=state_out.at[0, rows, columns],
            dst_ref=state.at[1, rows, columns],
            send_sem=state_send_sem.at[0, c],
            recv_sem=state_sem.at[1, c],
            device_id=(right,),
            device_id_type=MESH,
        )

    detour_start = starts[DETOUR_CHUNK] + CHUNKS[DETOUR_CHUNK] - DETOUR
    detour = pl.ds(detour_start, DETOUR)

    def send_direct():
        rows = pl.ds(starts[DETOUR_CHUNK], CHUNKS[DETOUR_CHUNK] - DETOUR)
        return pltpu.make_async_remote_copy(
            src_ref=state_out.at[0, rows],
            dst_ref=state.at[1, rows],
            send_sem=state_send_sem.at[0, DETOUR_CHUNK],
            recv_sem=state_sem.at[1, DETOUR_CHUNK],
            device_id=(right,),
            device_id_type=MESH,
        )

    def send_detour():
        return pltpu.make_async_remote_copy(
            src_ref=state_out.at[0, detour],
            dst_ref=relay,
            send_sem=state_send_sem.at[0, DETOUR_CHUNK],
            recv_sem=relay_sem,
            device_id=(first_relay,),
            device_id_type=MESH,
        )

    def pass_on():
        return pltpu.make_async_remote_copy(
            src_ref=relay,
            dst_ref=relay,
            send_sem=relay_send_sem,
            recv_sem=relay_sem,
            device_id=(second_relay,),
            device_id_type=MESH,
        )

    def deliver():
        return pltpu.make_async_remote_copy(
            src_ref=relay,
            dst_ref=state.at[1, detour],
            send_sem=relay_send_sem,
            recv_sem=state_sem.at[1, DETOUR_CHUNK],
            device_id=(end,),
            device_id_type=MESH,
        )

    def send_adjoint(sweep, c):
        rows = pl.ds(starts[c], CHUNKS[c])
        slot = lax.rem(sweep, 2)
        return pltpu.make_async_remote_copy(
            src_ref=adjoint_out.at[slot, rows],
            dst_ref=adjoint.at[sweep + 1, rows],
            send_sem=adjoint_send_sem.at[slot, c],
            recv_sem=adjoint_sem.at[sweep + 1, c],
            device_id=(left,),
            device_id_type=MESH,
        )

    def load_weights(t):
        rows = pl.ds(t * TILE, TILE)
        return pltpu.make_async_copy(
            weights_ref.at[0, rows], weights.at[rows], load_sem.at[1 + t]
        )

    load_gains = pltpu.make_async_copy(gains_ref, gains, load_sem.at[0])
    load_gains.start()
    load_state(0, 0).start()
    for t in range(tiles):
        load_weights(t).start()
    load_adjoint(0, 0).start()

    def load_the_rest():
        for c, _ in chunks[1:]:
            load_state(0, c).start()
            load_adjoint(0, c).start()

        @pl.when(me == 0)
        def _():
            for sweep in range(1, SWEEPS + 1):
                for c, _ in chunks:
                    load_state(sweep, c).start()

        @pl.when(me == n - 1)
        def _():
            for sweep in range(1, SWEEPS + 1):
                for c, _ in chunks:
                    load_adjoint(sweep, c).start()

    def forward(sweep, c, first, last):
        start, count = starts[c], CHUNKS[c]
        rows = pl.ds(start, count)
        load_state(sweep, c).wait()
        if first and c == 0:
            load_gains.wait()
        block = state[sweep, rows, :]
        inverse = lax.rsqrt(jnp.mean(block * block, axis=-1, keepdims=True) + EPS)
        unit = block * inverse
        normed[pl.ds(0, count), :] = unit
        scaled[rows, :] = (unit * gains[...]).astype(jnp.bfloat16)
        if first and c == 0:
            for t in range(tiles):
                load_weights(t).wait()
            load_the_rest()
        slot = lax.rem(sweep, 2)
        for t in range(tiles):
            columns = pl.ds(t * TILE, TILE)
            preact = jnp.dot(
                scaled[rows, :], weights[:, columns], preferred_element_type=jnp.float32
            )
            squash = 0.5 * jnp.tanh(0.5 * preact) + 0.5
            slope[pl.ds(0, count), columns] = squash * (1.0 + preact * (1.0 - squash))
            if not last:
                state_out[slot, rows, columns] = state[sweep, rows, columns] + preact * squash
            if first and c == 0:
                if t == 0:
                    more = jnp.logical_or(diverts, jnp.logical_or(relays_first, relays_second))
                    pl.semaphore_wait(barrier, jnp.where(more, 3, 2))

                @pl.when(me < n - 1)
                def _():
                    send_state_tile(c, t).start()
        return inverse

    def backward(sweep, c, inverse, last):
        start, count = starts[c], CHUNKS[c]
        rows = pl.ds(start, count)
        here = pl.ds(0, count)
        load_adjoint(sweep, c).wait()
        pre_grad[rows, :] = (adjoint[sweep, rows, :] * slope[here, :]).astype(jnp.bfloat16)
        slot = lax.rem(sweep, 2)
        projection = jnp.zeros((count, 1), jnp.float32)
        for t in range(tiles):
            columns = pl.ds(t * TILE, TILE)
            feat_grad = lax.dot_general(
                pre_grad[rows, :],
                weights[columns, :],
                (((1,), (1,)), ((), ())),
                preferred_element_type=jnp.float32,
            )
            if last:
                part = jnp.sum(normed[here, columns] * feat_grad, axis=0, keepdims=True)
                gain_total[:, columns] = part if c == 0 else gain_total[:, columns] + part
            else:
                gained = feat_grad * gains[:, columns]
                product[here, columns] = gained
                projection += jnp.sum(gained * normed[here, columns], axis=-1, keepdims=True)
        if not last:
            projection = projection / width
            adjoint_out[slot, rows, :] = adjoint[sweep, rows, :] + inverse * (
                product[here, :] - normed[here, :] * projection
            )

    def sweep_chunk(sweep, c, first):
        if not isinstance(sweep, int) or sweep >= 2:

            @pl.when(jnp.logical_and(sweep >= 2, me < n - 1))
            def _():
                send_state(sweep - 2, c).wait_send()

            @pl.when(jnp.logical_and(sweep >= 2, me > 0))
            def _():
                send_adjoint(sweep - 2, c).wait_send()

        inverse = forward(sweep, c, first, False)
        if first and c == DETOUR_CHUNK:

            @pl.when(diverts)
            def _():
                send_direct().start()
                send_detour().start()

            @pl.when(jnp.logical_and(me < n - 1, jnp.logical_not(diverts)))
            def _():
                send_state(sweep, c).start()

        elif not (first and c == 0):

            @pl.when(me < n - 1)
            def _():
                send_state(sweep, c).start()

        backward(sweep, c, inverse, False)

        @pl.when(me > 0)
        def _():
            send_adjoint(sweep, c).start()

    for c, _ in chunks:
        sweep_chunk(0, c, True)

    @pl.loop(1, SWEEPS)
    def _(sweep):
        for c, _ in chunks:
            sweep_chunk(sweep, c, False)
            if c == FIRST_AFTER:

                @pl.when(jnp.logical_and(sweep == 1, relays_first))
                def _():
                    pass_on().wait_recv()
                    pass_on().start()

            if c == SECOND_AFTER:

                @pl.when(jnp.logical_and(sweep == 1, relays_second))
                def _():
                    pass_on().wait_recv()
                    deliver().start()


    for c, (start, count) in chunks:
        rows = pl.ds(start, count)
        inverse = forward(SWEEPS, c, False, True)
        backward(SWEEPS, c, inverse, True)
        if start >= tokens - TAIL:
            here = pl.ds(start - (tokens - TAIL), count)
            scaled_tail[here, :] = scaled[rows, :]
            pre_grad_tail[here, :] = pre_grad[rows, :]
        else:
            for t in range(tiles):
                columns = pl.ds(t * TILE, TILE)
                part = lax.dot_general(
                    scaled[rows, columns],
                    pre_grad[rows, :],
                    (((0,), (0,)), ((), ())),
                    preferred_element_type=jnp.float32,
                )
                total[columns, :] = part if c == 0 else total[columns, :] + part

    @pl.when(relays_first)
    def _():
        pass_on().wait_send()

    @pl.when(relays_second)
    def _():
        deliver().wait_send()

    for sweep in range(SWEEPS - 2, SWEEPS):
        for c, _ in chunks:

            @pl.when(me < n - 1)
            def _():
                send_state(sweep, c).wait_send()

            @pl.when(me > 0)
            def _():
                send_adjoint(sweep, c).wait_send()


def finish(
    total,
    scaled_tail,
    pre_grad_tail,
    gain_total,
    grad_weight_ref,
    grad_gain_ref,
    result,
    result_sem,
    gain_sem,
):
    store_gain = pltpu.make_async_copy(gain_total, grad_gain_ref, gain_sem)
    store_gain.start()
    stores = []
    for t in range(total.shape[0] // STORE):
        columns = pl.ds(t * STORE, STORE)
        part = lax.dot_general(
            scaled_tail[:, columns],
            pre_grad_tail[...],
            (((0,), (0,)), ((), ())),
            preferred_element_type=jnp.float32,
        )
        result[columns, :] = (total[columns, :] + part).astype(jnp.bfloat16)
        store = pltpu.make_async_copy(
            result.at[columns], grad_weight_ref.at[0, columns], result_sem.at[t]
        )
        store.start()
        stores.append(store)
    for store in stores:
        store.wait()
    store_gain.wait()


def solution(mesh):
    n = mesh.shape["depth"]

    def step(weights, gains, states, adjoints):
        _, tokens, width = states.shape
        assert sum(CHUNKS) == tokens
        largest = max(CHUNKS)
        slots = pltpu.VMEM((SWEEPS + 1, tokens, width), jnp.float32)
        sent = pltpu.VMEM((2, tokens, width), jnp.float32)
        piece = pltpu.VMEM((largest, width), jnp.float32)
        whole = pltpu.VMEM((tokens, width), jnp.bfloat16)
        any_space = pl.BlockSpec(memory_space=pl.ANY)
        vmem = pl.BlockSpec(memory_space=pltpu.VMEM)
        parts = pl.pallas_call(
            functools.partial(kernel, n),
            out_shape=(
                pltpu.VMEM((width, width), jnp.float32),
                pltpu.VMEM((TAIL, width), jnp.bfloat16),
                pltpu.VMEM((TAIL, width), jnp.bfloat16),
                pltpu.VMEM((1, width), jnp.float32),
            ),
            in_specs=[pl.BlockSpec(memory_space=pltpu.HBM)] * 4,
            out_specs=(vmem,) * 4,
            scratch_shapes=[
                pltpu.VMEM((width, width), jnp.bfloat16),
                pltpu.VMEM((1, width), jnp.float32),
                slots,
                slots,
                sent,
                sent,
                piece,
                piece,
                piece,
                whole,
                whole,
                pltpu.SemaphoreType.DMA((1 + width // TILE,)),
                pltpu.SemaphoreType.DMA((SWEEPS + 1, len(CHUNKS))),
                pltpu.SemaphoreType.DMA((SWEEPS + 1, len(CHUNKS))),
                pltpu.SemaphoreType.DMA((2, len(CHUNKS))),
                pltpu.SemaphoreType.DMA((2, len(CHUNKS))),
                pltpu.VMEM((DETOUR, width), jnp.float32),
                pltpu.SemaphoreType.DMA,
                pltpu.SemaphoreType.DMA,
            ],
            compiler_params=pltpu.CompilerParams(
                collective_id=0, has_side_effects=True, vmem_limit_bytes=48 * 2**20
            ),
            cost_estimate=pl.CostEstimate(
                flops=2 * tokens * width * width * (2 * SWEEPS + 3),
                bytes_accessed=4 * width * width + 8 * tokens * width,
                transcendentals=tokens * width * (SWEEPS + 1),
            ),
        )(*(pltpu.with_memory_space_constraint(x, pltpu.HBM) for x in (weights, gains, states, adjoints)))
        return pl.pallas_call(
            finish,
            out_shape=(
                jax.ShapeDtypeStruct((1, width, width), jnp.bfloat16),
                jax.ShapeDtypeStruct((1, width), jnp.float32),
            ),
            in_specs=[vmem] * 4,
            out_specs=(any_space, any_space),
            scratch_shapes=[
                pltpu.VMEM((width, width), jnp.bfloat16),
                pltpu.SemaphoreType.DMA((width // STORE,)),
                pltpu.SemaphoreType.DMA,
            ],
            compiler_params=pltpu.CompilerParams(vmem_limit_bytes=24 * 2**20),
            cost_estimate=pl.CostEstimate(
                flops=2 * TAIL * width * width,
                bytes_accessed=6 * width * width,
                transcendentals=0,
            ),
        )(*parts)

    spec = P("depth", None, None)
    return jax.shard_map(
        step,
        mesh=mesh,
        in_specs=(spec, P("depth", None), spec, spec),
        out_specs=(spec, P("depth", None)),
        check_vma=False,
    )
```
